512 devices in a mesh: dp: 8 (over z_hi, x), context: 4 (over y), tensor: 16 (over z_lo, core).
Axes of the slice: x: 4, y: 4, z: 16 (z_hi: 2, z_lo: 8; z = z_hi * 8 + z_lo), core: 2. Of those that a mesh axis runs over, the one named last changes fastest.
Arguments:
- output_gradient: bfloat16 [8192, 4096], P(('dp', 'context', 'tensor')), may hold values from -6 to 6
- gate_preactivation: bfloat16 [8192, 16384], P(('dp', 'context'), 'tensor'), may hold values from -6 to 6
- up_preactivation: bfloat16 [8192, 16384], P(('dp', 'context'), 'tensor'), may hold values from -6 to 6
- router_scores_saved: float32 [8192, 8], P(('dp', 'context')), may hold values from -6 to 6
- router_input_rows: bfloat16 [8192, 4096], P(('dp', 'context', 'tensor')), may hold values from -6 to 6
- down_matrix: bfloat16 [16384, 4096], P('tensor', ('dp', 'context')), may hold values from -0.046875 to 0.046875
- adapter_first_factor: bfloat16 [16384, 512], P('tensor'), may hold values from -0.046875 to 0.046875
- adapter_second_factor: bfloat16 [512, 4096], P('tensor', ('dp', 'context')), may hold values from -0.25 to 0.25
Outputs:
- grad_gate: bfloat16 [8192, 16384], P(('dp', 'context'), 'tensor')
- grad_up: bfloat16 [8192, 16384], P(('dp', 'context'), 'tensor')
- router_grad: float32 [8, 4096], replicated
The draws below stay inside these ranges and needn't reach their ends.
All inputs are finite; a program needn't handle non-finite values.
Results may differ from the reference program's by a relative error of at most 0.005.
Values may be sent and summed in bfloat16 or wider, within the bound.
A program may use at most 64 MiB of HBM per device.

```python
import math
import jax
import jax.numpy as jnp
from jax import lax

MODEL_WIDTH = 4096
HIDDEN_UNITS = 16384
EXPERTS = 8
TOTAL_RANK = 512
TOKENS = 8192


def block_scale(own_key, dims, shards, smallest, top_value):
    factor_of = 1.0
    for dim, blocks in shards:
        draws = jax.random.uniform(jax.random.fold_in(jax.random.fold_in(own_key, 6), dim), (blocks,), jnp.float32, smallest / len(shards), top_value / len(shards))
        factor_of = factor_of * jnp.repeat(jnp.exp(draws), dims[dim] // blocks).reshape((-1,) + (1,) * (len(dims) - 1 - dim))
    return factor_of


def scatter_about(rng, dims, spread, most, shards=(), dtype=jnp.bfloat16):
    factor_of = block_scale(rng, dims, shards, -0.22, 0.18) if shards else 1.0
    result = jax.random.normal(rng, dims, jnp.float32) * spread * factor_of
    return jnp.minimum(jnp.maximum(result, -most), most).astype(dtype)


def setup_inputs(seed: int = 0) -> dict:
    seeds = jax.random.split(jax.random.key(seed), 9)
    return {
        "output_gradient": scatter_about(seeds[0], (TOKENS, MODEL_WIDTH), 1.0, 6.0, ((0, 512),)),
        "gate_preactivation": scatter_about(seeds[1], (TOKENS, HIDDEN_UNITS), 1.5, 6.0, ((0, 32), (1, 16))),
        "up_preactivation": scatter_about(seeds[2], (TOKENS, HIDDEN_UNITS), 1.0, 6.0, ((0, 32), (1, 16))),
        "router_scores_saved": scatter_about(seeds[3], (TOKENS, EXPERTS), 1.5, 6.0, ((0, 32),), jnp.float32),
        "router_input_rows": scatter_about(seeds[4], (TOKENS, MODEL_WIDTH), 1.0, 6.0, ((0, 512),)),
        "down_matrix": scatter_about(seeds[5], (HIDDEN_UNITS, MODEL_WIDTH), HIDDEN_UNITS ** -0.5, 0.046875, ((0, 16), (1, 32))),
        "adapter_first_factor": scatter_about(seeds[6], (HIDDEN_UNITS, TOTAL_RANK), HIDDEN_UNITS ** -0.5, 0.046875, ((0, 16),)),
        "adapter_second_factor": scatter_about(seeds[7], (TOTAL_RANK, MODEL_WIDTH), TOTAL_RANK ** -0.5, 0.25, ((0, 16), (1, 32))),
    }


def reference(output_gradient, gate_preactivation, up_preactivation, router_scores_saved, router_input_rows, down_matrix, adapter_first_factor, adapter_second_factor):
    gate_vals = gate_preactivation.astype(jnp.float32)
    up_vals = up_preactivation.astype(jnp.float32)
    sigmoid_gate = jax.nn.sigmoid(gate_vals)
    hidden_state = (gate_vals * sigmoid_gate * up_vals).astype(jnp.bfloat16)
    gate_probs = jax.nn.sigmoid(router_scores_saved)
    tokens, experts = gate_probs.shape
    combined_rank = adapter_first_factor.shape[1]
    per_expert = combined_rank // experts
    rank_scale = jnp.broadcast_to(gate_probs[:, :, None], (tokens, experts, per_expert)).reshape(tokens, combined_rank)
    contracting_dimensions = (((1,), (1,)), ((), ()))
    middle_state = jnp.dot(hidden_state, adapter_first_factor, preferred_element_type=jnp.float32)
    lowrank_gradient = lax.dot_general(output_gradient, adapter_second_factor, contracting_dimensions, preferred_element_type=jnp.float32).astype(jnp.bfloat16)
    middle_gradient = (lowrank_gradient.astype(jnp.float32) * rank_scale).astype(jnp.bfloat16)
    hidden_gradient = lax.dot_general(output_gradient, down_matrix, contracting_dimensions, preferred_element_type=jnp.float32)
    hidden_gradient = hidden_gradient + lax.dot_general(middle_gradient, adapter_first_factor, contracting_dimensions, preferred_element_type=jnp.float32)
    grad_up = (hidden_gradient * gate_vals * sigmoid_gate).astype(jnp.bfloat16)
    grad_gate = (hidden_gradient * up_vals * sigmoid_gate * (1.0 + gate_vals * (1.0 - sigmoid_gate))).astype(jnp.bfloat16)
    grad_probs = (middle_state * lowrank_gradient.astype(jnp.float32)).reshape(tokens, experts, per_expert).sum(-1)
    grad_logits = grad_probs * gate_probs * (1.0 - gate_probs)
    router_grad = lax.dot_general(grad_logits, router_input_rows.astype(jnp.float32), (((0,), (0,)), ((), ())), precision=lax.Precision.HIGHEST)
    router_grad = router_grad / math.sqrt(TOKENS)
    return (grad_gate, grad_up, router_grad)
```

```python
import math

import jax
import jax.numpy as jnp
from jax import lax
from jax.experimental import pallas as pl
from jax.experimental.pallas import tpu as pltpu
from jax.sharding import PartitionSpec as P

MESH = pl.DeviceIdType.MESH
NT = (((1,), (1,)), ((), ()))
BF = jnp.bfloat16
F32 = jnp.float32
HI = lax.Precision.HIGHEST
QORDER = (0, 2, 1, 3)


def iota(shape, dim):
    return lax.broadcasted_iota(jnp.int32, shape, dim)


def kernel(
    scale,
    og_ref, gate_ref, up_ref, scores_ref, rows_ref, down_ref, first_ref, second_ref,
    gg_ref, gu_ref, rg_ref,
    wb, gb, a2b, gate, up, first, rows, hid, su, sg, mid, rs, pr, acc, lowb,
    qs, qs_in, qo, qr, rpb, rs_in, t1, rx, t2, ry, rz, fin,
    in_sem, w_send, w_recv, wz_recv,
    g_send, gsib_send, g_recv, gsib_recv,
    a2_send, a2z_recv, a2y_recv, a2x_recv,
    low_send, low_recv, q_send, q_recv,
    r_send, rs_recv, rx_recv, ry_recv, rz_recv, ay_recv, ax_recv, as_recv,
):
    dp = lax.axis_index("dp")
    y = lax.axis_index("context")
    ten = lax.axis_index("tensor")
    zh, x = dp // 4, dp % 4
    zl, c = ten // 2, ten % 2
    z = zh * 8 + zl
    oc = 1 - c

    def at_x(d):
        return (zh * 4 + (x + d + 4) % 4, y, ten)

    def at_y(d):
        return (dp, (y + d + 4) % 4, ten)

    def at_z(d):
        zz = (z + d + 16) % 16
        return ((zz // 8) * 4 + x, y, (zz % 8) * 2 + c)

    def at_zl(l):
        return (dp, y, l * 2 + c)

    sibling = (dp, y, zl * 2 + oc)

    def rc(src, dst, ss, rsm, dev):
        return pltpu.make_async_remote_copy(
            src_ref=src, dst_ref=dst, send_sem=ss, recv_sem=rsm, device_id=dev, device_id_type=MESH
        )

    def arrived(ref, sem):
        rc(ref, ref, w_send, sem, sibling).wait_recv()

    def sent(ref, sem):
        rc(ref, ref, sem, as_recv, sibling).wait_send()

    own_slot = (zh * 4 + x) * 4 + y
    my_rows = pl.ds(pl.multiple_of(ten * 16, 16), 16)

    ins = [
        pltpu.make_async_copy(og_ref, gb.at[my_rows], in_sem.at[0]),
        pltpu.make_async_copy(down_ref, wb.at[own_slot], in_sem.at[1]),
        pltpu.make_async_copy(second_ref, a2b.at[own_slot], in_sem.at[2]),
        pltpu.make_async_copy(gate_ref, gate, in_sem.at[3]),
        pltpu.make_async_copy(up_ref, up, in_sem.at[4]),
        pltpu.make_async_copy(first_ref, first, in_sem.at[5]),
        pltpu.make_async_copy(rows_ref, rows, in_sem.at[6]),
    ]
    for cp in ins:
        cp.start()

    peers = [sibling] + [at_x(d) for d in (1, 2, 3)] + [at_y(d) for d in (1, 2, 3)]
    peers += [at_z(d) for d in range(1, 16)]
    barrier = pltpu.get_barrier_semaphore()
    for dev in peers:
        pl.semaphore_signal(barrier, inc=1, device_id=dev, device_id_type=MESH)

    ins[3].wait()
    ins[4].wait()

    @pl.loop(0, 8)
    def _(i):
        r = pl.ds(pl.multiple_of(i * 32, 32), 32)
        g = gate[r, :].astype(F32)
        u = up[r, :].astype(F32)
        s = jax.nn.sigmoid(g)
        gs = g * s
        hid[r, :] = (gs * u).astype(BF)
        su[r, :] = gs
        sg[r, :] = u * s * (1.0 + g * (1.0 - s))

    ins[0].wait()
    ins[1].wait()
    ins[2].wait()
    pl.semaphore_wait(barrier, len(peers))

    def g_part(l, core, h):
        return gb.at[pl.ds(pl.multiple_of((l * 2 + core) * 16, 16), 16), pl.ds(h * 2048, 2048)]

    def g_block(l, core):
        return gb.at[pl.ds(pl.multiple_of((l * 2 + core) * 16, 16), 16)]

    def g_forward(l, h, to):
        rc(g_part(l, c, h), g_part(l, c, h), g_send, g_recv.at[l * 2 + h], at_zl(to)).start()

    def g_sibling(l):
        rc(g_block(l, c), g_block(l, c), gsib_send, gsib_recv.at[l], sibling).start()

    for h in range(2):
        @pl.when(zl < 7)
        def _():
            g_forward(zl, h, zl + 1)

        @pl.when(zl > 0)
        def _():
            g_forward(zl, h, zl - 1)

    def a2_y(zz):
        for d in (1, 2, 3):
            slot = (zz * 4 + x) * 4 + y
            rc(a2b.at[slot], a2b.at[slot], a2_send, a2y_recv.at[zz * 4 + y], at_y(d)).start()

    def a2_x(zz):
        for d in (1, 2, 3):
            slot = (zz * 4 + (x + d) % 4) * 4
            yy = (y + d) % 4
            arrived(a2b.at[(zz * 4 + x) * 4 + yy], a2y_recv.at[zz * 4 + yy])
        four = a2b.at[pl.ds((zz * 4 + x) * 4, 4)]
        for d in (1, 2, 3):
            rc(four, four, a2_send, a2x_recv.at[zz * 4 + x], at_x(d)).start()

    def a2_done(zz):
        for d in (1, 2, 3):
            xx = (x + d) % 4
            arrived(a2b.at[pl.ds((zz * 4 + xx) * 4, 4)], a2x_recv.at[zz * 4 + xx])

    zo = 1 - zh
    oth_slot = (zo * 4 + x) * 4 + y
    rc(a2b.at[own_slot], a2b.at[own_slot], a2_send, a2z_recv, at_z(8)).start()
    a2_y(zh)

    def w_part(slot, q):
        return wb.at[slot, pl.ds(q * 256, 256)]

    def place(zz, q, da, db):
        xx, yy = (x + da, y + db) if q < 2 else (x + db, y + da)
        return (zz * 4 + (xx + 4) % 4) * 4 + (yy + 4) % 4

    def w_send_to(slot, q, along, d):
        first_axis_x = q < 2
        dev = at_x(d) if (along == 0) == first_axis_x else at_y(d)
        rc(w_part(slot, q), w_part(slot, q), w_send, w_recv.at[slot * 4 + q], dev).start()

    def w_wait(slot, q):
        arrived(w_part(slot, q), w_recv.at[slot * 4 + q])

    def e0(zz, q):
        s = place(zz, q, 0, 0)
        w_send_to(s, q, 0, 1)
        w_send_to(s, q, 0, -1)
        w_send_to(s, q, 1, 1)
        w_send_to(s, q, 1, -1)

    def e1(zz, q):
        for da in (-1, 1):
            s = place(zz, q, da, 0)
            w_wait(s, q)
            if da == (-1 if q % 2 == 0 else 1):
                w_send_to(s, q, 0, -da)
            w_send_to(s, q, 1, 1)
            w_send_to(s, q, 1, -1)

    def e2(zz, q):
        s = place(zz, q, 2, 0)
        w_wait(s, q)
        w_send_to(s, q, 1, 1)
        w_send_to(s, q, 1, -1)

    def e3(zz, q, das):
        for da in das:
            for db in (-1, 1):
                s = place(zz, q, da, db)
                w_wait(s, q)
                if db == (-1 if q % 2 == 0 else 1):
                    w_send_to(s, q, 1, -db)

    def e4(zz, q):
        for da in (0, -1, 1, 2):
            w_wait(place(zz, q, da, 2), q)

    for q in QORDER:
        e0(zh, q)
    g_sibling(zl)
    for q in QORDER:
        rc(w_part(own_slot, q), w_part(own_slot, q), w_send, wz_recv.at[q], at_z(8)).start()

    p = jax.nn.sigmoid(scores_ref[...])
    lane = iota((256, 512), 1) // 64
    scale_rows = jnp.broadcast_to(p[:, 0:1], (256, 512))
    for e in range(1, 8):
        scale_rows = jnp.where(lane == e, p[:, e : e + 1], scale_rows)
    rs[...] = scale_rows
    lane = iota((256, 128), 1) // 16
    p16 = jnp.broadcast_to(p[:, 0:1], (256, 128))
    for e in range(1, 8):
        p16 = jnp.where(lane == e, p[:, e : e + 1], p16)
    same = iota((256, 128), 0) % 16 == iota((256, 128), 1) % 16
    pr[...] = jnp.where(same, p16 * (1.0 - p16), 0.0)
    ins[5].wait()
    ins[6].wait()

    def g_step(s):
        for sign in (-1, 1):
            l = zl + sign * s
            ok = (l >= 0) if sign < 0 else (l <= 7)
            more = (zl < 7) if sign < 0 else (zl > 0)

            @pl.when(ok)
            def _():
                for h in range(2):
                    arrived(g_part(l, c, h), g_recv.at[l * 2 + h])

                    @pl.when(more)
                    def _():
                        g_forward(l, h, zl - sign)
                g_sibling(l)

    for q in QORDER:
        e1(zh, q)
    g_step(1)
    a2_x(zh)
    for q in QORDER:
        e3(zh, q, (0,))
    g_step(2)
    for q in QORDER:
        e2(zh, q)
    g_step(3)
    arrived(a2b.at[oth_slot], a2z_recv)
    a2_y(zo)
    for q in QORDER:
        e3(zh, q, (-1, 1))
    for n in range(2):
        mid[:, 256 * n : 256 * n + 256] = jnp.dot(
            hid[...], first[:, 256 * n : 256 * n + 256], preferred_element_type=F32
        )
    g_step(4)
    a2_x(zo)
    for q in QORDER:
        e3(zh, q, (2,))
    g_step(5)
    a2_done(zh)
    g_step(6)
    a2_done(zo)
    g_step(7)

    def z_in(q):
        arrived(w_part(oth_slot, q), wz_recv.at[q])
        e0(zo, q)

    z_in(0)
    z_in(2)

    for d in range(8):
        arrived(g_block(d, oc), gsib_recv.at[d])

    def low_group(i, tot):
        a = jnp.concatenate([a2b[i * 4 + k] for k in range(4)], axis=1)
        g = gb[:, pl.ds(pl.multiple_of(i * 512, 512), 512)]
        return tot + lax.dot_general(a, g, NT, preferred_element_type=F32)

    lowb[ten] = lax.fori_loop(0, 8, low_group, jnp.zeros((32, 256), F32)).astype(BF)

    def low_out(j, dev):
        rc(lowb.at[j], lowb.at[j], low_send, low_recv.at[j], dev).start()

    for d in range(1, 8):
        low_out(ten, at_zl((zl + d) % 8))
    low_out(ten, sibling)

    z_in(1)
    z_in(3)
    for q in QORDER:
        e4(zh, q)

    def base_tile(zz, n):
        tot = None
        for k in range(4):
            w = jnp.concatenate(
                [wb[zz * 16 + k * 4 + i, pl.ds(pl.multiple_of(n * 256, 256), 256), :] for i in range(4)], axis=1
            )
            g = gb[:, pl.ds(pl.multiple_of(zz * 2048 + k * 512, 512), 512)]
            t = lax.dot_general(g, w, NT, preferred_element_type=F32)
            tot = t if tot is None else tot + t
        return tot

    @pl.loop(0, 4)
    def _(n):
        acc[:, pl.ds(pl.multiple_of(n * 256, 256), 256)] = base_tile(zh, n)

    for q in (0, 2):
        e1(zo, q)
    for d in range(1, 8):
        j = ((zl + d) % 8) * 2 + c
        arrived(lowb.at[j], low_recv.at[j])
        low_out(j, sibling)
    for q in (1, 3):
        e1(zo, q)
    for q in QORDER:
        e3(zo, q, (0,))
    for d in range(8):
        j = d * 2 + oc
        arrived(lowb.at[j], low_recv.at[j])

    low = jnp.transpose(lowb[...].reshape(512, 256).astype(F32))
    pm = mid[...] * low
    spread = jnp.where(iota((512, 128), 0) // 64 == iota((512, 128), 1) // 16, 1.0, 0.0)
    part = jnp.dot(pm, spread, precision=HI, preferred_element_type=F32) * pr[...]
    pick = jnp.where(iota((16, 256), 1) // 16 == iota((16, 256), 0), 1.0, 0.0)
    qs[...] = jnp.dot(pick, part, precision=HI, preferred_element_type=F32)
    rc(qs, qs_in, q_send.at[0], q_recv.at[8], sibling).start()
    hid[:, 0:512] = (low * rs[...]).astype(BF)

    for q in QORDER:
        e2(zo, q)
    arrived(qs_in, q_recv.at[8])
    both = qs[...] + qs_in[...]
    for l in range(8):
        row = jnp.where(c == 0, both[2 * l : 2 * l + 1], both[2 * l + 1 : 2 * l + 2])
        qo[l] = jnp.broadcast_to(row, (8, 128))
    qr[zl] = qo[zl]
    for d in range(1, 8):
        l = (zl + d) % 8
        rc(qo.at[l], qr.at[zl], q_send.at[1], q_recv.at[zl], at_zl(l)).start()

    for n in range(4):
        acc[:, 256 * n : 256 * n + 256] += lax.dot_general(
            hid[:, 0:512], first[256 * n : 256 * n + 256, :], NT, preferred_element_type=F32
        )
    for q in QORDER:
        e3(zo, q, (-1, 1))

    for d in range(1, 8):
        l = (zl + d) % 8
        arrived(qr.at[l], q_recv.at[l])
    lsum = qr[0]
    for l in range(1, 8):
        lsum = lsum + qr[l]
    lmat = jnp.where(iota((8, 128), 0) == iota((8, 128), 1) // 16, lsum, 0.0)
    fold = jnp.where(iota((128, 16), 0) % 16 == iota((128, 16), 1), 1.0, 0.0)
    l2 = jnp.dot(lmat, fold, precision=HI, preferred_element_type=F32)
    for k in range(4):
        t = jnp.dot(l2, rows[:, 1024 * k : 1024 * k + 1024].astype(F32), precision=HI, preferred_element_type=F32)
        for i in range(8):
            rpb[k * 8 + i] = t[:, 128 * i : 128 * i + 128]
    rc(rpb.at[pl.ds(oc * 16, 16)], rs_in, r_send.at[0], rs_recv, sibling).start()
    for q in QORDER:
        e3(zo, q, (2,))
    arrived(rs_in, rs_recv)
    t1[...] = rpb[pl.ds(c * 16, 16)] + rs_in[...]
    for d in (1, 2, 3):
        rc(t1.at[pl.ds(((x + d) % 4) * 4, 4)], rx.at[x], r_send.at[1], rx_recv.at[x], at_x(d)).start()
    rx[x] = t1[pl.ds(x * 4, 4)]
    for d in (1, 2, 3):
        xx = (x + d) % 4
        arrived(rx.at[xx], rx_recv.at[xx])
    t2[...] = rx[0] + rx[1] + rx[2] + rx[3]
    for d in (1, 2, 3):
        rc(t2.at[(y + d) % 4], ry.at[y], r_send.at[2], ry_recv.at[y], at_y(d)).start()
    ry[y] = t2[y]
    for d in (1, 2, 3):
        yy = (y + d) % 4
        arrived(ry.at[yy], ry_recv.at[yy])
    rz[z] = ry[0] + ry[1] + ry[2] + ry[3]
    for d in range(1, 16):
        rc(rz.at[z], rz.at[z], r_send.at[3], rz_recv.at[z], at_z(d)).start()

    for q in range(4):
        e4(zo, q)
        cols = slice(256 * q, 256 * q + 256)
        hg = acc[:, cols] + base_tile(zo, q)
        gu_ref[:, cols] = (hg * su[:, cols]).astype(BF)
        gg_ref[:, cols] = (hg * sg[:, cols]).astype(BF)

    for d in range(1, 16):
        zz = (z + d) % 16
        arrived(rz.at[zz], rz_recv.at[zz])
    tot = rz[0]
    for l in range(1, 16):
        tot = tot + rz[l]
    piece = c * 16 + x * 4 + y
    fin[piece] = tot / scale
    for d in (1, 2, 3):
        rc(fin.at[piece], fin.at[piece], r_send.at[4], ay_recv.at[y], at_y(d)).start()
    for d in (1, 2, 3):
        yy = (y + d) % 4
        arrived(fin.at[c * 16 + x * 4 + yy], ay_recv.at[yy])
    four = fin.at[pl.ds(c * 16 + x * 4, 4)]
    for d in (1, 2, 3):
        rc(four, four, r_send.at[5], ax_recv.at[x], at_x(d)).start()
    for d in (1, 2, 3):
        xx = (x + d) % 4
        arrived(fin.at[pl.ds(c * 16 + xx * 4, 4)], ax_recv.at[xx])
    half = fin.at[pl.ds(c * 16, 16)]
    rc(half, half, r_send.at[6], as_recv, sibling).start()
    arrived(fin.at[pl.ds(oc * 16, 16)], as_recv)
    for i in range(32):
        rg_ref[:, 128 * i : 128 * i + 128] = fin[i]

    sent(wb.at[pl.ds(0, 31)], w_send)
    sent(gb.at[pl.ds(0, 128)], gsib_send)
    inner = jnp.logical_and(zl > 0, zl < 7)

    @pl.when(inner)
    def _():
        sent(gb.at[pl.ds(0, 144)], g_send)

    @pl.when(jnp.logical_not(inner))
    def _():
        sent(gb.at[pl.ds(0, 16)], g_send)

    sent(a2b.at[pl.ds(0, 31)], a2_send)
    sent(lowb.at[pl.ds(0, 15)], low_send)
    sent(qs, q_send.at[0])
    sent(qo.at[pl.ds(0, 7)], q_send.at[1])
    for i, n in enumerate((16, 12, 3, 15, 3, 12, 16)):
        sent(rpb.at[pl.ds(0, n)], r_send.at[i])


def local(og, gate, up, scores, rows, down, first, second):
    tokens = gate.shape[0] * lax.axis_size("dp") * lax.axis_size("context")
    anywhere = pl.BlockSpec(memory_space=pl.ANY)
    vmem = pl.BlockSpec(memory_space=pltpu.VMEM)
    dma = pltpu.SemaphoreType.DMA
    V = pltpu.VMEM

    def body(*refs):
        kernel(math.sqrt(tokens), *refs)

    return pl.pallas_call(
        body,
        out_shape=(
            jax.ShapeDtypeStruct((256, 1024), BF),
            jax.ShapeDtypeStruct((256, 1024), BF),
            jax.ShapeDtypeStruct((8, 4096), F32),
        ),
        in_specs=[anywhere, anywhere, anywhere, vmem, anywhere, anywhere, anywhere, anywhere],
        out_specs=(vmem, vmem, vmem),
        scratch_shapes=[
            V((32, 1024, 128), BF), V((256, 4096), BF), V((32, 32, 128), BF),
            V((256, 1024), BF), V((256, 1024), BF), V((1024, 512), BF), V((16, 4096), BF),
            V((256, 1024), BF), V((256, 1024), F32), V((256, 1024), F32), V((256, 512), F32),
            V((256, 512), F32), V((256, 128), F32), V((256, 1024), F32), V((16, 32, 256), BF),
            V((16, 128), F32), V((16, 128), F32), V((8, 8, 128), F32), V((8, 8, 128), F32),
            V((32, 8, 128), F32), V((16, 8, 128), F32), V((16, 8, 128), F32), V((4, 4, 8, 128), F32),
            V((4, 8, 128), F32), V((4, 8, 128), F32), V((16, 8, 128), F32), V((32, 8, 128), F32),
            dma((7,)), dma, dma((128,)), dma((4,)),
            dma, dma, dma((16,)), dma((8,)),
            dma, dma, dma((8,)), dma((8,)),
            dma, dma((16,)), dma((2,)), dma((9,)),
            dma((7,)), dma, dma((4,)), dma((4,)), dma((16,)), dma((4,)), dma((4,)), dma,
        ],
        compiler_params=pltpu.CompilerParams(
            collective_id=0, has_side_effects=True, vmem_limit_bytes=48 * 2**20
        ),
        cost_estimate=pl.CostEstimate(flops=3 * 10**9, bytes_accessed=4 * 2**20, transcendentals=2**18),
        name="swiglu_down_backward",
    )(og, gate, up, scores, rows, down, first, second)


def solution(mesh):
    return jax.shard_map(
        local,
        mesh=mesh,
        in_specs=(
            P(("dp", "context", "tensor"), None),
            P(("dp", "context"), "tensor"),
            P(("dp", "context"), "tensor"),
            P(("dp", "context"), None),
            P(("dp", "context", "tensor"), None),
            P("tensor", ("dp", "context")),
            P("tensor", None),
            P("tensor", ("dp", "context")),
        ),
        out_specs=(P(("dp", "context"), "tensor"), P(("dp", "context"), "tensor"), P()),
        check_vma=False,
    )
```

```python
import math

import jax
import jax.numpy as jnp
from jax import lax
from jax.experimental import pallas as pl
from jax.experimental.pallas import tpu as pltpu
from jax.sharding import PartitionSpec as P

MESH = pl.DeviceIdType.MESH
NT = (((1,), (1,)), ((), ()))
BF = jnp.bfloat16
F32 = jnp.float32
HI = lax.Precision.HIGHEST
QORDER = (0, 2, 1, 3)
GSUB = 4
GW = 4096 // GSUB


def iota(shape, dim):
    return lax.broadcasted_iota(jnp.int32, shape, dim)


def kernel(
    scale,
    og_ref, gate_ref, up_ref, scores_ref, rows_ref, down_ref, first_ref, second_ref,
    gg_ref, gu_ref, rg_ref,
    wb, gb, a2b, gate, up, first, rows, hid, su, sg, rs, pd, acc, lowb, lowf,
    mid, mid_in, mid_sum, mid_got, rpb, rs_in, t1, rx, rz, fin,
    in_sem, w_send, w_recv, wz_recv,
    g_send, gsib_send, g_recv, gsib_recv,
    a2_send, a2z_recv, a2y_recv, a2x_recv,
    low_send, low_recv, m_send, m_recv,
    r_send, rs_recv, rx_recv, rz_recv, ay_recv, as_recv,
):
    dp = lax.axis_index("dp")
    y = lax.axis_index("context")
    ten = lax.axis_index("tensor")
    zh, x = dp // 4, dp % 4
    zl, c = ten // 2, ten % 2
    z = zh * 8 + zl
    oc = 1 - c

    def at_x(d):
        return (zh * 4 + (x + d + 4) % 4, y, ten)

    def at_y(d):
        return (dp, (y + d + 4) % 4, ten)

    def at_z(d):
        zz = (z + d + 16) % 16
        return ((zz // 8) * 4 + x, y, (zz % 8) * 2 + c)

    def at_zl(l):
        return (dp, y, l * 2 + c)

    sibling = (dp, y, zl * 2 + oc)

    def rc(src, dst, ss, rsm, dev):
        return pltpu.make_async_remote_copy(
            src_ref=src, dst_ref=dst, send_sem=ss, recv_sem=rsm, device_id=dev, device_id_type=MESH
        )

    def arrived(ref, sem):
        rc(ref, ref, w_send, sem, sibling).wait_recv()

    def sent(ref, sem):
        rc(ref, ref, sem, as_recv, sibling).wait_send()

    own_slot = (zh * 4 + x) * 4 + y
    my_rows = pl.ds(pl.multiple_of(ten * 16, 16), 16)

    ins = [
        pltpu.make_async_copy(og_ref, gb.at[my_rows], in_sem.at[0]),
        pltpu.make_async_copy(down_ref, wb.at[own_slot], in_sem.at[1]),
        pltpu.make_async_copy(second_ref, a2b.at[own_slot], in_sem.at[2]),
        pltpu.make_async_copy(gate_ref, gate, in_sem.at[3]),
        pltpu.make_async_copy(up_ref, up, in_sem.at[4]),
        pltpu.make_async_copy(first_ref, first, in_sem.at[5]),
        pltpu.make_async_copy(rows_ref, rows, in_sem.at[6]),
    ]
    for cp in ins:
        cp.start()

    peers = [sibling]
    peers += [(zh * 4 + (x + i) % 4, (y + j) % 4, ten) for i in range(4) for j in range(4) if i or j]
    peers += [at_z(d) for d in range(1, 16)]
    barrier = pltpu.get_barrier_semaphore()
    for dev in peers:
        pl.semaphore_signal(barrier, inc=1, device_id=dev, device_id_type=MESH)

    ins[3].wait()
    ins[4].wait()

    @pl.loop(0, 8)
    def _(i):
        r = pl.ds(pl.multiple_of(i * 32, 32), 32)
        g = gate[r, :].astype(F32)
        u = up[r, :].astype(F32)
        s = jax.nn.sigmoid(g)
        gs = g * s
        hid[r, :] = (gs * u).astype(BF)
        su[r, :] = gs
        sg[r, :] = u * s * (1.0 + g * (1.0 - s))


    p = jax.nn.sigmoid(jnp.transpose(scores_ref[...]))
    lane = iota((256, 512), 1) // 64
    scale_rows = jnp.broadcast_to(p[:, 0:1], (256, 512))
    for e in range(1, 8):
        scale_rows = jnp.where(lane == e, p[:, e : e + 1], scale_rows)
    rs[...] = scale_rows
    pd[...] = p * (1.0 - p)
    ins[5].wait()
    for n in range(2):
        cols = slice(256 * n, 256 * n + 256)
        part = jnp.dot(hid[...], first[:, cols], preferred_element_type=F32)
        for j in range(16):
            mid[j % 2, j // 2, :, cols] = part[16 * j : 16 * j + 16]
    ins[0].wait()
    ins[1].wait()
    ins[2].wait()
    ins[6].wait()
    pl.semaphore_wait(barrier, len(peers))

    def g_part(l, core, h):
        return gb.at[pl.ds(pl.multiple_of((l * 2 + core) * 16, 16), 16), pl.ds(h * GW, GW)]

    def g_block(l, core):
        return gb.at[pl.ds(pl.multiple_of((l * 2 + core) * 16, 16), 16)]

    def g_forward(l, h, to):
        rc(g_part(l, c, h), g_part(l, c, h), g_send, g_recv.at[l * GSUB + h], at_zl(to)).start()

    def g_sibling(l):
        rc(g_block(l, c), g_block(l, c), gsib_send, gsib_recv.at[l], sibling).start()

    def g_start():
        for h in range(GSUB):
            @pl.when(zl < 7)
            def _():
                g_forward(zl, h, zl + 1)

            @pl.when(zl > 0)
            def _():
                g_forward(zl, h, zl - 1)
        g_sibling(zl)

    def a2_y(zz):
        for d in (1, 2, 3):
            slot = (zz * 4 + x) * 4 + y
            rc(a2b.at[slot], a2b.at[slot], a2_send, a2y_recv.at[zz * 4 + y], at_y(d)).start()

    def a2_x(zz):
        for d in (1, 2, 3):
            slot = (zz * 4 + (x + d) % 4) * 4
            yy = (y + d) % 4
            arrived(a2b.at[(zz * 4 + x) * 4 + yy], a2y_recv.at[zz * 4 + yy])
        four = a2b.at[pl.ds((zz * 4 + x) * 4, 4)]
        for d in (1, 2, 3):
            rc(four, four, a2_send, a2x_recv.at[zz * 4 + x], at_x(d)).start()

    def a2_done(zz):
        for d in (1, 2, 3):
            xx = (x + d) % 4
            arrived(a2b.at[pl.ds((zz * 4 + xx) * 4, 4)], a2x_recv.at[zz * 4 + xx])

    zo = 1 - zh
    oth_slot = (zo * 4 + x) * 4 + y

    def a2_start():
        a2_y(zh)
        rc(a2b.at[own_slot], a2b.at[own_slot], a2_send, a2z_recv, at_z(8)).start()

    def a2_in():
        arrived(a2b.at[oth_slot], a2z_recv)
        a2_y(zo)

    def w_part(slot, q):
        return wb.at[slot, pl.ds(q * 256, 256)]

    def place(zz, q, da, db):
        xx, yy = (x + da, y + db) if q < 2 else (x + db, y + da)
        return (zz * 4 + (xx + 4) % 4) * 4 + (yy + 4) % 4

    def w_send_to(slot, q, along, d):
        first_axis_x = q < 2
        dev = at_x(d) if (along == 0) == first_axis_x else at_y(d)
        rc(w_part(slot, q), w_part(slot, q), w_send, w_recv.at[slot * 4 + q], dev).start()

    def w_wait(slot, q):
        arrived(w_part(slot, q), w_recv.at[slot * 4 + q])

    def e0(zz, q):
        s = place(zz, q, 0, 0)
        w_send_to(s, q, 0, 1)
        w_send_to(s, q, 0, -1)
        w_send_to(s, q, 1, 1)
        w_send_to(s, q, 1, -1)

    def e1(zz, q):
        for da in (-1, 1):
            s = place(zz, q, da, 0)
            w_wait(s, q)
            if da == (-1 if q % 2 == 0 else 1):
                w_send_to(s, q, 0, -da)
            w_send_to(s, q, 1, 1)
            w_send_to(s, q, 1, -1)

    def e2(zz, q):
        s = place(zz, q, 2, 0)
        w_wait(s, q)
        w_send_to(s, q, 1, 1)
        w_send_to(s, q, 1, -1)

    def e3(zz, q, das):
        for da in das:
            for db in (-1, 1):
                s = place(zz, q, da, db)
                w_wait(s, q)
                if db == (-1 if q % 2 == 0 else 1):
                    w_send_to(s, q, 1, -db)

    def e4(zz, q):
        for da in (0, -1, 1, 2):
            w_wait(place(zz, q, da, 2), q)

    def z_out(q):
        rc(w_part(own_slot, q), w_part(own_slot, q), w_send, wz_recv.at[q], at_z(8)).start()

    def z_in(q):
        arrived(w_part(oth_slot, q), wz_recv.at[q])
        e0(zo, q)

    def e13(zz, q):
        e1(zz, q)
        e3(zz, q, (0,))

    def g_step(s):
        steps = []
        for sign in (-1, 1):
            l = zl + sign * s
            ok = (l >= 0) if sign < 0 else (l <= 7)
            more = jnp.logical_and(ok, (zl < 7) if sign < 0 else (zl > 0))
            steps.append((sign, l, ok, more))
        for h in range(GSUB):
            for sign, l, ok, more in steps:
                @pl.when(ok)
                def _():
                    arrived(g_part(l, c, h), g_recv.at[l * GSUB + h])

                @pl.when(more)
                def _():
                    g_forward(l, h, zl - sign)

        for sign, l, ok, more in steps:
            @pl.when(ok)
            def _():
                g_sibling(l)

    def mid_pair():
        rc(mid.at[oc], mid_in, m_send.at[0], m_recv.at[8], sibling).start()

    def mid_out():
        arrived(mid_in, m_recv.at[8])
        mid_sum[...] = (mid[c] + mid_in[...]).astype(BF)
        for d in range(1, 8):
            l = (zl + d) % 8
            rc(mid_sum.at[l], mid_got.at[zl], m_send.at[1], m_recv.at[zl], at_zl(l)).start()
        mid_got[zl] = mid_sum[zl]

    def low_out(j, dev):
        rc(lowb.at[j], lowb.at[j], low_send, low_recv.at[j], dev).start()

    def low_own():
        a2_done(zh)
        a2_done(zo)
        for d in range(8):
            arrived(g_block(d, oc), gsib_recv.at[d])

        def low_group(i, tot):
            a = jnp.concatenate([a2b[i * 4 + k] for k in range(4)], axis=1)
            g = gb[:, pl.ds(pl.multiple_of(i * 512, 512), 512)]
            return tot + lax.dot_general(a, g, NT, preferred_element_type=F32)

        lowb[ten] = lax.fori_loop(0, 8, low_group, jnp.zeros((32, 256), F32)).astype(BF)
        for d in range(1, 8):
            low_out(ten, at_zl((zl + d) % 8))
        low_out(ten, sibling)

    def low_pass():
        for d in range(1, 8):
            j = ((zl + d) % 8) * 2 + c
            arrived(lowb.at[j], low_recv.at[j])
            low_out(j, sibling)

    def low_use():
        for d in range(8):
            j = d * 2 + oc
            arrived(lowb.at[j], low_recv.at[j])
        lowf[...] = jnp.transpose(lowb[...].reshape(512, 256).astype(F32))
        for d in range(1, 8):
            l = (zl + d) % 8
            arrived(mid_got.at[l], m_recv.at[l])
        middle = mid_got[0].astype(F32)
        for l in range(1, 8):
            middle = middle + mid_got[l].astype(F32)
        prod = middle * lowf[my_rows]
        spread = jnp.where(iota((8, 512), 1) // 64 == iota((8, 512), 0), 1.0, 0.0)
        eye = jnp.where(iota((8, 8), 0) == iota((8, 8), 1), 1.0, 0.0)
        probs = lax.dot_general(spread, prod, NT, precision=HI, preferred_element_type=F32)
        slope = lax.dot_general(eye, pd[my_rows], NT, precision=HI, preferred_element_type=F32)
        logits = probs * slope
        for k in range(4):
            part = jnp.dot(
                logits, rows[:, 1024 * k : 1024 * k + 1024].astype(F32), precision=HI, preferred_element_type=F32
            )
            for i in range(8):
                rpb[k * 8 + i] = part[:, 128 * i : 128 * i + 128]
        rc(rpb.at[pl.ds(oc * 16, 16)], rs_in, r_send.at[0], rs_recv, sibling).start()
        hid[:, 0:512] = (lowf[...] * rs[...]).astype(BF)

    def low_rank_term():
        for n in range(4):
            acc[:, 256 * n : 256 * n + 256] += lax.dot_general(
                hid[:, 0:512], first[256 * n : 256 * n + 256, :], NT, preferred_element_type=F32
            )

    def base_tile(zz, n):
        tot = None
        for k in range(4):
            w = jnp.concatenate(
                [wb[zz * 16 + k * 4 + i, pl.ds(n * 256, 256), :] for i in range(4)], axis=1
            )
            g = gb[:, pl.ds(pl.multiple_of(zz * 2048 + k * 512, 512), 512)]
            t = lax.dot_general(g, w, NT, preferred_element_type=F32)
            tot = t if tot is None else tot + t
        return tot

    def base_own(q):
        e4(zh, q)
        acc[:, 256 * q : 256 * q + 256] = base_tile(zh, q)

    def base_other(q):
        e4(zo, q)
        cols = slice(256 * q, 256 * q + 256)
        hg = acc[:, cols] + base_tile(zo, q)
        gu_ref[:, cols] = (hg * su[:, cols]).astype(BF)
        gg_ref[:, cols] = (hg * sg[:, cols]).astype(BF)

    here = x * 4 + y
    piece = c * 16 + here
    around = [(dx, dy) for dx in range(4) for dy in range(4) if dx or dy]

    def at_xy(dx, dy):
        return (zh * 4 + (x + dx) % 4, (y + dy) % 4, ten)

    def place_xy(dx, dy):
        return ((x + dx) % 4) * 4 + (y + dy) % 4

    def router_p():
        arrived(rs_in, rs_recv)
        t1[...] = rpb[pl.ds(c * 16, 16)] + rs_in[...]
        for d in around:
            rc(t1.at[place_xy(*d)], rx.at[here], r_send.at[1], rx_recv.at[here], at_xy(*d)).start()
        rx[here] = t1[here]

    def router_z():
        for d in around:
            arrived(rx.at[place_xy(*d)], rx_recv.at[place_xy(*d)])
        tot = rx[0]
        for l in range(1, 16):
            tot = tot + rx[l]
        rz[z] = tot
        for d in range(1, 16):
            rc(rz.at[z], rz.at[z], r_send.at[2], rz_recv.at[z], at_z(d)).start()

    def router_back_p():
        for d in range(1, 16):
            zz = (z + d) % 16
            arrived(rz.at[zz], rz_recv.at[zz])
        tot = rz[0]
        for l in range(1, 16):
            tot = tot + rz[l]
        fin[piece] = tot / scale
        for d in around:
            rc(fin.at[piece], fin.at[piece], r_send.at[3], ay_recv.at[here], at_xy(*d)).start()

    def router_back():
        for d in around:
            arrived(fin.at[c * 16 + place_xy(*d)], ay_recv.at[place_xy(*d)])
        half = fin.at[pl.ds(c * 16, 16)]
        rc(half, half, r_send.at[4], as_recv, sibling).start()

    def router_end():
        arrived(fin.at[pl.ds(oc * 16, 16)], as_recv)
        for i in range(32):
            rg_ref[:, 128 * i : 128 * i + 128] = fin[i]

    g_start()
    a2_start()
    mid_pair()
    e0(zh,0)
    e0(zh,2)
    e0(zh,1)
    e0(zh,3)
    g_step(1)
    a2_x(zh)
    e13(zh,0)
    e13(zh,2)
    g_step(2)
    e13(zh,1)
    e13(zh,3)
    g_step(3)
    e2(zh,0)
    e2(zh,2)
    a2_in()
    g_step(4)
    e2(zh,1)
    e2(zh,3)
    a2_x(zo)
    g_step(5)
    mid_out()
    e3(zh,0,(-1,1))
    e3(zh,2,(-1,1))
    e3(zh,1,(-1,1))
    e3(zh,3,(-1,1))
    g_step(6)
    z_out(0)
    e3(zh,0,(2,))
    e3(zh,2,(2,))
    g_step(7)
    z_out(2)
    e3(zh,1,(2,))
    e3(zh,3,(2,))
    low_own()
    z_out(1)
    base_own(0)
    base_own(2)
    base_own(1)
    base_own(3)
    low_pass()
    low_use()
    z_out(3)
    z_in(0)
    z_in(2)
    router_p()
    e13(zo,0)
    e13(zo,2)
    router_z()
    z_in(1)
    e2(zo,0)
    e2(zo,2)
    e3(zo,0,(-1,1))
    e3(zo,2,(-1,1))
    z_in(3)
    e13(zo,1)
    e13(zo,3)
    e3(zo,0,(2,))
    e3(zo,2,(2,))
    low_rank_term()
    router_back_p()
    e2(zo,1)
    e2(zo,3)
    e3(zo,1,(-1,1))
    e3(zo,3,(-1,1))
    router_back()
    base_other(0)
    base_other(2)
    e3(zo,1,(2,))
    e3(zo,3,(2,))
    router_end()
    base_other(1)
    base_other(3)

    sent(wb.at[pl.ds(0, 31)], w_send)
    sent(gb.at[pl.ds(0, 128)], gsib_send)
    inner = jnp.logical_and(zl > 0, zl < 7)

    @pl.when(inner)
    def _():
        sent(gb.at[pl.ds(0, 144)], g_send)

    @pl.when(jnp.logical_not(inner))
    def _():
        sent(gb.at[pl.ds(0, 16)], g_send)

    sent(a2b.at[pl.ds(0, 31)], a2_send)
    sent(lowb.at[pl.ds(0, 15)], low_send)
    sent(mid_in, m_send.at[0])
    sent(mid_sum.at[pl.ds(0, 7)], m_send.at[1])
    for i, n in enumerate((16, 15, 15, 15, 16)):
        sent(rpb.at[pl.ds(0, n)], r_send.at[i])


def local(og, gate, up, scores, rows, down, first, second):
    tokens = gate.shape[0] * lax.axis_size("dp") * lax.axis_size("context")
    anywhere = pl.BlockSpec(memory_space=pl.ANY)
    vmem = pl.BlockSpec(memory_space=pltpu.VMEM)
    dma = pltpu.SemaphoreType.DMA
    V = pltpu.VMEM

    def body(*refs):
        kernel(math.sqrt(tokens), *refs)

    return pl.pallas_call(
        body,
        out_shape=(
            jax.ShapeDtypeStruct((256, 1024), BF),
            jax.ShapeDtypeStruct((256, 1024), BF),
            jax.ShapeDtypeStruct((8, 4096), F32),
        ),
        in_specs=[anywhere, anywhere, anywhere, vmem, anywhere, anywhere, anywhere, anywhere],
        out_specs=(vmem, vmem, vmem),
        scratch_shapes=[
            V((32, 1024, 128), BF), V((256, 4096), BF), V((32, 32, 128), BF),
            V((256, 1024), BF), V((256, 1024), BF), V((1024, 512), BF), V((16, 4096), BF),
            V((256, 1024), BF), V((256, 1024), F32), V((256, 1024), F32), V((256, 512), F32),
            V((256, 8), F32), V((256, 1024), F32), V((16, 32, 256), BF), V((256, 512), F32),
            V((2, 8, 16, 512), F32), V((8, 16, 512), F32), V((8, 16, 512), BF), V((8, 16, 512), BF),
            V((32, 8, 128), F32), V((16, 8, 128), F32), V((16, 8, 128), F32), V((16, 8, 128), F32),
            V((16, 8, 128), F32), V((32, 8, 128), F32),
            dma((7,)), dma, dma((128,)), dma((4,)),
            dma, dma, dma((8 * GSUB,)), dma((8,)),
            dma, dma, dma((8,)), dma((8,)),
            dma, dma((16,)), dma((2,)), dma((9,)),
            dma((5,)), dma, dma((16,)), dma((16,)), dma((16,)), dma,
        ],
        compiler_params=pltpu.CompilerParams(
            collective_id=0, has_side_effects=True, vmem_limit_bytes=62 * 2**20
        ),
        cost_estimate=pl.CostEstimate(flops=3 * 10**9, bytes_accessed=4 * 2**20, transcendentals=2**18),
        name="swiglu_down_backward",
    )(og, gate, up, jnp.transpose(scores), rows, down, first, second)


def solution(mesh):
    return jax.shard_map(
        local,
        mesh=mesh,
        in_specs=(
            P(("dp", "context", "tensor"), None),
            P(("dp", "context"), "tensor"),
            P(("dp", "context"), "tensor"),
            P(("dp", "context"), None),
            P(("dp", "context", "tensor"), None),
            P("tensor", ("dp", "context")),
            P("tensor", None),
            P("tensor", ("dp", "context")),
        ),
        out_specs=(P(("dp", "context"), "tensor"), P(("dp", "context"), "tensor"), P()),
        check_vma=False,
    )
```

```python
import math

import jax
import jax.numpy as jnp
from jax import lax
from jax.experimental import pallas as pl
from jax.experimental.pallas import tpu as pltpu
from jax.sharding import PartitionSpec as P

MESH = pl.DeviceIdType.MESH
NT = (((1,), (1,)), ((), ()))
BF = jnp.bfloat16
F32 = jnp.float32
HI = lax.Precision.HIGHEST
QORDER = (0, 2, 1, 3)
GSUB = 4
GW = 4096 // GSUB


def iota(shape, dim):
    return lax.broadcasted_iota(jnp.int32, shape, dim)


def kernel(
    scale,
    og_ref, gate_ref, up_ref, scores_ref, rows_ref, down_ref, first_ref, second_ref,
    gg_ref, gu_ref, rg_ref,
    wb, gb, a2l, gs, gx, lp, lr, gate, up, first, rows, hid, su, sg, rs, pd, acc, lowb,
    mid, mid_in, mid_sum, mid_got, rpb, rs_in, t1, rx, rz, fin,
    in_sem, w_send, w_recv, wz_recv,
    g_send, gsib_send, g_recv, gsib_recv,
    a2z_send, a2z_recv, a2_send, a2_recv, gx_send, gx_recv, lp_send, lp_recv,
    low_send, low_recv, m_send, m_recv,
    r_send, rs_recv, rx_recv, rz_recv, ay_recv, as_recv,
):
    dp = lax.axis_index("dp")
    y = lax.axis_index("context")
    ten = lax.axis_index("tensor")
    zh, x = dp // 4, dp % 4
    zl, c = ten // 2, ten % 2
    z = zh * 8 + zl
    oc = 1 - c

    def at_x(d):
        return (zh * 4 + (x + d + 4) % 4, y, ten)

    def at_y(d):
        return (dp, (y + d + 4) % 4, ten)

    def at_z(d):
        zz = (z + d + 16) % 16
        return ((zz // 8) * 4 + x, y, (zz % 8) * 2 + c)

    def at_zl(l):
        return (dp, y, l * 2 + c)

    sibling = (dp, y, zl * 2 + oc)

    def rc(src, dst, ss, rsm, dev):
        return pltpu.make_async_remote_copy(
            src_ref=src, dst_ref=dst, send_sem=ss, recv_sem=rsm, device_id=dev, device_id_type=MESH
        )

    def arrived(ref, sem):
        rc(ref, ref, w_send, sem, sibling).wait_recv()

    def sent(ref, sem):
        rc(ref, ref, sem, as_recv, sibling).wait_send()

    own_slot = (zh * 4 + x) * 4 + y
    my_rows = pl.ds(pl.multiple_of(ten * 16, 16), 16)

    ins = [
        pltpu.make_async_copy(og_ref, gb.at[my_rows], in_sem.at[0]),
        pltpu.make_async_copy(down_ref, wb.at[own_slot], in_sem.at[1]),
        pltpu.make_async_copy(second_ref, a2l.at[ten, zh], in_sem.at[2]),
        pltpu.make_async_copy(gate_ref, gate, in_sem.at[3]),
        pltpu.make_async_copy(up_ref, up, in_sem.at[4]),
        pltpu.make_async_copy(first_ref, first, in_sem.at[5]),
        pltpu.make_async_copy(rows_ref, rows, in_sem.at[6]),
    ]
    for cp in ins:
        cp.start()

    peers = [sibling]
    peers += [(zh * 4 + (x + i) % 4, (y + j) % 4, ten) for i in range(4) for j in range(4) if i or j]
    peers += [at_z(d) for d in range(1, 16)]
    barrier = pltpu.get_barrier_semaphore()
    for dev in peers:
        pl.semaphore_signal(barrier, inc=1, device_id=dev, device_id_type=MESH)

    ins[3].wait()
    ins[4].wait()

    @pl.loop(0, 8)
    def _(i):
        r = pl.ds(pl.multiple_of(i * 32, 32), 32)
        g = gate[r, :].astype(F32)
        u = up[r, :].astype(F32)
        s = jax.nn.sigmoid(g)
        gs = g * s
        hid[r, :] = (gs * u).astype(BF)
        su[r, :] = gs
        sg[r, :] = u * s * (1.0 + g * (1.0 - s))


    p = jax.nn.sigmoid(jnp.transpose(scores_ref[...]))
    lane = iota((256, 512), 1) // 64
    scale_rows = jnp.broadcast_to(p[:, 0:1], (256, 512))
    for e in range(1, 8):
        scale_rows = jnp.where(lane == e, p[:, e : e + 1], scale_rows)
    rs[...] = scale_rows
    pd[...] = p * (1.0 - p)
    ins[5].wait()
    for n in range(2):
        cols = slice(256 * n, 256 * n + 256)
        part = jnp.dot(hid[...], first[:, cols], preferred_element_type=F32)
        for j in range(16):
            mid[j % 2, j // 2, :, cols] = part[16 * j : 16 * j + 16]
    ins[0].wait()
    ins[1].wait()
    ins[2].wait()
    ins[6].wait()
    pl.semaphore_wait(barrier, len(peers))

    def g_part(l, core, h):
        return gb.at[pl.ds(pl.multiple_of((l * 2 + core) * 16, 16), 16), pl.ds(h * GW, GW)]

    def g_block(l, core):
        return gb.at[pl.ds(pl.multiple_of((l * 2 + core) * 16, 16), 16)]

    def g_forward(l, h, to):
        rc(g_part(l, c, h), g_part(l, c, h), g_send, g_recv.at[l * GSUB + h], at_zl(to)).start()

    def g_sibling(l):
        rc(g_block(l, c), g_block(l, c), gsib_send, gsib_recv.at[l], sibling).start()

    def g_start():
        for h in range(GSUB):
            @pl.when(zl < 7)
            def _():
                g_forward(zl, h, zl + 1)

            @pl.when(zl > 0)
            def _():
                g_forward(zl, h, zl - 1)
        g_sibling(zl)

    here = x * 4 + y
    piece = c * 16 + here
    around = [(dx, dy) for dx in range(4) for dy in range(4) if dx or dy]

    def at_xy(dx, dy):
        return (zh * 4 + (x + dx) % 4, (y + dy) % 4, ten)

    def place_xy(dx, dy):
        return ((x + dx) % 4) * 4 + (y + dy) % 4

    zo = 1 - zh
    oth_slot = (zo * 4 + x) * 4 + y

    def a2_z():
        rc(a2l.at[ten, zh], a2l.at[ten, zh], a2z_send, a2z_recv, at_z(8)).start()

    def a2_out(j, dev):
        rc(a2l.at[j], a2l.at[j], a2_send, a2_recv.at[j], dev).start()

    def a2_line():
        arrived(a2l.at[ten, zo], a2z_recv)
        for d in range(1, 8):
            a2_out(ten, at_zl((zl + d) % 8))
        a2_out(ten, sibling)

    def a2_pass():
        for d in range(1, 8):
            j = ((zl + d) % 8) * 2 + c
            arrived(a2l.at[j], a2_recv.at[j])
            a2_out(j, sibling)

    def gx_out():
        block = gb[my_rows, :]
        for i in range(16):
            for k in range(2):
                s = (k * 16 + i) * 128
                gs[i, k] = block[:, s : s + 128]
        for d in around:
            rc(gs.at[place_xy(*d)], gx.at[here], gx_send, gx_recv.at[here], at_xy(*d)).start()
        gx[here] = gs[here]

    def low_part():
        for d in around:
            arrived(gx.at[place_xy(*d)], gx_recv.at[place_xy(*d)])
        for l in range(8):
            arrived(a2l.at[l * 2 + oc], a2_recv.at[l * 2 + oc])
        g = jnp.concatenate([gx[:, k].reshape(256, 128) for k in range(2)], axis=1)
        for n in range(2):
            a = jnp.concatenate([a2l[8 * n : 8 * n + 8, k].reshape(256, 128) for k in range(2)], axis=1)
            r = lax.dot_general(g, a, NT, preferred_element_type=F32)
            lp[:, :, 256 * n : 256 * n + 256] = r.reshape(16, 16, 256)
        for d in around:
            rc(lp.at[place_xy(*d)], lr.at[here], lp_send, lp_recv.at[here], at_xy(*d)).start()
        lr[here] = lp[here]

    def w_part(slot, q):
        return wb.at[slot, pl.ds(q * 256, 256)]

    def place(zz, q, da, db):
        xx, yy = (x + da, y + db) if q < 2 else (x + db, y + da)
        return (zz * 4 + (xx + 4) % 4) * 4 + (yy + 4) % 4

    def w_send_to(slot, q, along, d):
        first_axis_x = q < 2
        dev = at_x(d) if (along == 0) == first_axis_x else at_y(d)
        rc(w_part(slot, q), w_part(slot, q), w_send, w_recv.at[slot * 4 + q], dev).start()

    def w_wait(slot, q):
        arrived(w_part(slot, q), w_recv.at[slot * 4 + q])

    def e0(zz, q):
        s = place(zz, q, 0, 0)
        w_send_to(s, q, 0, 1)
        w_send_to(s, q, 0, -1)
        w_send_to(s, q, 1, 1)
        w_send_to(s, q, 1, -1)

    def e1(zz, q):
        for da in (-1, 1):
            s = place(zz, q, da, 0)
            w_wait(s, q)
            if da == (-1 if q % 2 == 0 else 1):
                w_send_to(s, q, 0, -da)
            w_send_to(s, q, 1, 1)
            w_send_to(s, q, 1, -1)

    def e2(zz, q):
        s = place(zz, q, 2, 0)
        w_wait(s, q)
        w_send_to(s, q, 1, 1)
        w_send_to(s, q, 1, -1)

    def e3(zz, q, das):
        for da in das:
            for db in (-1, 1):
                s = place(zz, q, da, db)
                w_wait(s, q)
                if db == (-1 if q % 2 == 0 else 1):
                    w_send_to(s, q, 1, -db)

    def e4(zz, q):
        for da in (0, -1, 1, 2):
            w_wait(place(zz, q, da, 2), q)

    def z_out(q):
        rc(w_part(own_slot, q), w_part(own_slot, q), w_send, wz_recv.at[q], at_z(8)).start()

    def z_in(q):
        arrived(w_part(oth_slot, q), wz_recv.at[q])
        e0(zo, q)

    def e13(zz, q):
        e1(zz, q)
        e3(zz, q, (0,))

    def g_step(s):
        steps = []
        for sign in (-1, 1):
            l = zl + sign * s
            ok = (l >= 0) if sign < 0 else (l <= 7)
            more = jnp.logical_and(ok, (zl < 7) if sign < 0 else (zl > 0))
            steps.append((sign, l, ok, more))
        for h in range(GSUB):
            for sign, l, ok, more in steps:
                @pl.when(ok)
                def _():
                    arrived(g_part(l, c, h), g_recv.at[l * GSUB + h])

                @pl.when(more)
                def _():
                    g_forward(l, h, zl - sign)

        for sign, l, ok, more in steps:
            @pl.when(ok)
            def _():
                g_sibling(l)

    def mid_pair():
        rc(mid.at[oc], mid_in, m_send.at[0], m_recv.at[8], sibling).start()

    def mid_out():
        arrived(mid_in, m_recv.at[8])
        mid_sum[...] = (mid[c] + mid_in[...]).astype(BF)
        for d in range(1, 8):
            l = (zl + d) % 8
            rc(mid_sum.at[l], mid_got.at[zl], m_send.at[1], m_recv.at[zl], at_zl(l)).start()
        mid_got[zl] = mid_sum[zl]

    def low_out(j, dev):
        rc(lowb.at[j], lowb.at[j], low_send, low_recv.at[j], dev).start()

    def low_sum():
        for d in around:
            arrived(lr.at[place_xy(*d)], lp_recv.at[place_xy(*d)])
        tot = lr[0]
        for l in range(1, 16):
            tot = tot + lr[l]
        own = tot.astype(BF)
        lowb[ten] = own
        for d in range(1, 8):
            low_out(ten, at_zl((zl + d) % 8))
        low_out(ten, sibling)
        for d in range(1, 8):
            l = (zl + d) % 8
            arrived(mid_got.at[l], m_recv.at[l])
        middle = mid_got[0].astype(F32)
        for l in range(1, 8):
            middle = middle + mid_got[l].astype(F32)
        prod = middle * own.astype(F32)
        spread = jnp.where(iota((8, 512), 1) // 64 == iota((8, 512), 0), 1.0, 0.0)
        eye = jnp.where(iota((8, 8), 0) == iota((8, 8), 1), 1.0, 0.0)
        probs = lax.dot_general(spread, prod, NT, precision=HI, preferred_element_type=F32)
        slope = lax.dot_general(eye, pd[my_rows], NT, precision=HI, preferred_element_type=F32)
        logits = probs * slope
        for k in range(4):
            part = jnp.dot(
                logits, rows[:, 1024 * k : 1024 * k + 1024].astype(F32), precision=HI, preferred_element_type=F32
            )
            for i in range(8):
                rpb[k * 8 + i] = part[:, 128 * i : 128 * i + 128]
        rc(rpb.at[pl.ds(oc * 16, 16)], rs_in, r_send.at[0], rs_recv, sibling).start()

    def low_pass():
        for d in range(1, 8):
            j = ((zl + d) % 8) * 2 + c
            arrived(lowb.at[j], low_recv.at[j])
            low_out(j, sibling)

    def low_use():
        for d in range(8):
            j = d * 2 + oc
            arrived(lowb.at[j], low_recv.at[j])
        low = lowb[...].reshape(256, 512).astype(F32)
        hid[:, 0:512] = (low * rs[...]).astype(BF)

    def g_done():
        for d in range(8):
            arrived(g_block(d, oc), gsib_recv.at[d])

    def low_rank_term():
        for n in range(4):
            acc[:, 256 * n : 256 * n + 256] += lax.dot_general(
                hid[:, 0:512], first[256 * n : 256 * n + 256, :], NT, preferred_element_type=F32
            )

    def base_tile(zz, n):
        tot = None
        for k in range(4):
            w = jnp.concatenate(
                [wb[zz * 16 + k * 4 + i, pl.ds(n * 256, 256), :] for i in range(4)], axis=1
            )
            g = gb[:, pl.ds(pl.multiple_of(zz * 2048 + k * 512, 512), 512)]
            t = lax.dot_general(g, w, NT, preferred_element_type=F32)
            tot = t if tot is None else tot + t
        return tot

    def base_own(q):
        e4(zh, q)
        acc[:, 256 * q : 256 * q + 256] = base_tile(zh, q)

    def base_other(q):
        e4(zo, q)
        cols = slice(256 * q, 256 * q + 256)
        hg = acc[:, cols] + base_tile(zo, q)
        gu_ref[:, cols] = (hg * su[:, cols]).astype(BF)
        gg_ref[:, cols] = (hg * sg[:, cols]).astype(BF)

    def router_p():
        arrived(rs_in, rs_recv)
        t1[...] = rpb[pl.ds(c * 16, 16)] + rs_in[...]
        for d in around:
            rc(t1.at[place_xy(*d)], rx.at[here], r_send.at[1], rx_recv.at[here], at_xy(*d)).start()
        rx[here] = t1[here]

    def router_z():
        for d in around:
            arrived(rx.at[place_xy(*d)], rx_recv.at[place_xy(*d)])
        tot = rx[0]
        for l in range(1, 16):
            tot = tot + rx[l]
        rz[z] = tot
        for d in range(1, 16):
            rc(rz.at[z], rz.at[z], r_send.at[2], rz_recv.at[z], at_z(d)).start()

    def router_back_p():
        for d in range(1, 16):
            zz = (z + d) % 16
            arrived(rz.at[zz], rz_recv.at[zz])
        tot = rz[0]
        for l in range(1, 16):
            tot = tot + rz[l]
        fin[piece] = tot / scale
        for d in around:
            rc(fin.at[piece], fin.at[piece], r_send.at[3], ay_recv.at[here], at_xy(*d)).start()

    def router_back():
        for d in around:
            arrived(fin.at[c * 16 + place_xy(*d)], ay_recv.at[place_xy(*d)])
        half = fin.at[pl.ds(c * 16, 16)]
        rc(half, half, r_send.at[4], as_recv, sibling).start()

    def router_end():
        arrived(fin.at[pl.ds(oc * 16, 16)], as_recv)
        for i in range(32):
            rg_ref[:, 128 * i : 128 * i + 128] = fin[i]

    a2_z()
    gx_out()
    z_out(0)
    z_out(2)
    z_out(1)
    z_out(3)
    mid_pair()
    e0(zh,0)
    e0(zh,2)
    e0(zh,1)
    e0(zh,3)
    e13(zh,0)
    e13(zh,2)
    a2_line()
    e13(zh,1)
    e13(zh,3)
    e2(zh,0)
    e2(zh,2)
    e2(zh,1)
    e2(zh,3)
    g_start()
    e3(zh,0,(-1,1))
    e3(zh,2,(-1,1))
    e3(zh,1,(-1,1))
    e3(zh,3,(-1,1))
    mid_out()
    a2_pass()
    e3(zh,0,(2,))
    e3(zh,2,(2,))
    e3(zh,1,(2,))
    e3(zh,3,(2,))
    low_part()
    g_step(1)
    z_in(0)
    z_in(2)
    low_sum()
    z_in(1)
    z_in(3)
    e13(zo,0)
    e13(zo,2)
    g_step(2)
    router_p()
    e13(zo,1)
    e13(zo,3)
    g_step(3)
    e2(zo,0)
    e2(zo,2)
    e2(zo,1)
    e2(zo,3)
    router_z()
    g_step(4)
    e3(zo,0,(-1,1))
    e3(zo,2,(-1,1))
    e3(zo,1,(-1,1))
    e3(zo,3,(-1,1))
    low_pass()
    g_step(5)
    e3(zo,0,(2,))
    e3(zo,2,(2,))
    e3(zo,1,(2,))
    e3(zo,3,(2,))
    g_step(6)
    low_use()
    g_step(7)
    router_back_p()
    g_done()
    base_own(0)
    base_own(1)
    base_own(2)
    base_own(3)
    low_rank_term()
    router_back()
    base_other(0)
    base_other(1)
    base_other(2)
    base_other(3)
    router_end()

    sent(wb.at[pl.ds(0, 31)], w_send)
    sent(gb.at[pl.ds(0, 128)], gsib_send)
    inner = jnp.logical_and(zl > 0, zl < 7)

    @pl.when(inner)
    def _():
        sent(gb.at[pl.ds(0, 144)], g_send)

    @pl.when(jnp.logical_not(inner))
    def _():
        sent(gb.at[pl.ds(0, 16)], g_send)

    sent(a2l.at[0, 0], a2z_send)
    sent(a2l.at[pl.ds(0, 15)], a2_send)
    sent(gs.at[pl.ds(0, 15)], gx_send)
    sent(lp.at[pl.ds(0, 15)], lp_send)
    sent(lowb.at[pl.ds(0, 15)], low_send)
    sent(mid_in, m_send.at[0])
    sent(mid_sum.at[pl.ds(0, 7)], m_send.at[1])
    for i, n in enumerate((16, 15, 15, 15, 16)):
        sent(rpb.at[pl.ds(0, n)], r_send.at[i])


def local(og, gate, up, scores, rows, down, first, second):
    tokens = gate.shape[0] * lax.axis_size("dp") * lax.axis_size("context")
    anywhere = pl.BlockSpec(memory_space=pl.ANY)
    vmem = pl.BlockSpec(memory_space=pltpu.VMEM)
    dma = pltpu.SemaphoreType.DMA
    V = pltpu.VMEM

    def body(*refs):
        kernel(math.sqrt(tokens), *refs)

    return pl.pallas_call(
        body,
        out_shape=(
            jax.ShapeDtypeStruct((256, 1024), BF),
            jax.ShapeDtypeStruct((256, 1024), BF),
            jax.ShapeDtypeStruct((8, 4096), F32),
        ),
        in_specs=[anywhere, anywhere, anywhere, vmem, anywhere, anywhere, anywhere, anywhere],
        out_specs=(vmem, vmem, vmem),
        scratch_shapes=[
            V((32, 1024, 128), BF), V((256, 4096), BF), V((16, 2, 32, 128), BF),
            V((16, 2, 16, 128), BF), V((16, 2, 16, 128), BF), V((16, 16, 512), F32), V((16, 16, 512), F32),
            V((256, 1024), BF), V((256, 1024), BF), V((1024, 512), BF), V((16, 4096), BF),
            V((256, 1024), BF), V((256, 1024), F32), V((256, 1024), F32), V((256, 512), F32),
            V((256, 8), F32), V((256, 1024), F32), V((16, 16, 512), BF),
            V((2, 8, 16, 512), F32), V((8, 16, 512), F32), V((8, 16, 512), BF), V((8, 16, 512), BF),
            V((32, 8, 128), F32), V((16, 8, 128), F32), V((16, 8, 128), F32), V((16, 8, 128), F32),
            V((16, 8, 128), F32), V((32, 8, 128), F32),
            dma((7,)), dma, dma((128,)), dma((4,)),
            dma, dma, dma((8 * GSUB,)), dma((8,)),
            dma, dma, dma, dma((16,)), dma, dma((16,)), dma, dma((16,)),
            dma, dma((16,)), dma((2,)), dma((9,)),
            dma((5,)), dma, dma((16,)), dma((16,)), dma((16,)), dma,
        ],
        compiler_params=pltpu.CompilerParams(
            collective_id=0, has_side_effects=True, vmem_limit_bytes=62 * 2**20
        ),
        cost_estimate=pl.CostEstimate(flops=3 * 10**9, bytes_accessed=4 * 2**20, transcendentals=2**18),
        name="swiglu_down_backward",
    )(og, gate, up, jnp.transpose(scores), rows, down, first, second)


def solution(mesh):
    return jax.shard_map(
        local,
        mesh=mesh,
        in_specs=(
            P(("dp", "context", "tensor"), None),
            P(("dp", "context"), "tensor"),
            P(("dp", "context"), "tensor"),
            P(("dp", "context"), None),
            P(("dp", "context", "tensor"), None),
            P("tensor", ("dp", "context")),
            P("tensor", None),
            P("tensor", ("dp", "context")),
        ),
        out_specs=(P(("dp", "context"), "tensor"), P(("dp", "context"), "tensor"), P()),
        check_vma=False,
    )
```
